32 devices in a mesh: groups: 2 (over x), row: 16 (over z, y, core).
Axes of the slice: x: 2, y: 2, z: 4, core: 2. Of those that a mesh axis runs over, the one named last changes fastest.
Arguments:
- pair: bfloat16 [256, 128, 128], P('groups', 'row'), parts along dimension 0, may hold values from -6 to 6
- residue_mask: int32 [256], P('groups'), parts along dimension 0, may hold values 0 or 1
- ln_in_gain: float32 [128], replicated, may hold values from 0.1 to 1.9
- ln_in_bias: float32 [128], replicated, may hold values from -1.5 to 1.5
- w_edges: bfloat16 [128, 256], replicated, may hold values from -0.5 to 0.5
- w_edge_gates: bfloat16 [128, 256], replicated, may hold values from -0.5 to 0.5
- ln_out_gain: float32 [128], replicated, may hold values from 0.1 to 1.9
- ln_out_bias: float32 [128], replicated, may hold values from -1.5 to 1.5
- w_gate: bfloat16 [128, 128], replicated, may hold values from -0.5 to 0.5
- w_out: bfloat16 [128, 128], replicated, may hold values from -0.5 to 0.5
Outputs:
- update: bfloat16 [256, 128, 128], P('groups', 'row'), parts along dimension 0
The draws below stay inside these ranges and needn't reach their ends.
There are 2 independent parts, one for each index of `groups`. The reference program is written for one: setup_inputs(seed, part) draws one part's arguments, and reference() takes and returns one part's arrays. A program takes and returns all parts, laid end to end along the dimension named above; an argument that names none is the same for every part. Nothing has to cross between parts.
All inputs are finite; a program needn't handle non-finite values.
Results may differ from the reference program's by a relative error of at most 0.0072.
Values may be sent and summed in bfloat16 or wider, within the bound.
No kernel may reach another device: no remote copies, remote signals or barrier semaphores. Data moves between devices by JAX's collectives and lax.ppermute only.
A program may use at most 128 MiB of HBM per device.

```python
import jax
import jax.numpy as jnp
from jax import lax

C_Z = 128
C_HID = 128
N = 128


def touch_ends(result, own_key, smallest, high):
    longest = result.shape.index(max(result.shape))
    spots = []
    for shift in (0, 1):
        where = [jax.random.randint(jax.random.fold_in(own_key, axis), (), 0, length) for axis, length in enumerate(result.shape)]
        where[longest] = (where[longest] + shift) % result.shape[longest]
        spots.append(tuple(where))
    return result.at[spots[0]].set(smallest).at[spots[1]].set(high)


def levels(stream_key, dims, split, least, top_value):
    level = 1.0
    for position, blocks in split:
        heights = jax.random.uniform(jax.random.fold_in(jax.random.fold_in(stream_key, 6), position), (blocks,), jnp.float32, least / len(split), top_value / len(split))
        level = level * jnp.repeat(jnp.exp(heights), dims[position] // blocks).reshape((-1,) + (1,) * (len(dims) - 1 - position))
    return level


def bell_draw(rng, extent, deviation, limit, split=(), held_as=jnp.bfloat16):
    entries = jax.random.normal(rng, extent, jnp.float32) * deviation
    if len(split) > 0:
        entries = levels(rng, extent, split, -0.22, 0.18) * entries
    return jnp.clip(entries, min=-limit, max=limit).astype(held_as)


def setup_inputs(seed: int = 0, part: int = 0) -> dict:
    keys = jax.random.split(jax.random.key(seed), 11)
    part_keys = jax.random.split(jax.random.fold_in(keys[10], part), 11)
    return {
        "pair": bell_draw(part_keys[0], (N, N, C_Z), 1.0, 6.0, ((1, 16),)),
        "residue_mask": touch_ends((jax.random.randint(part_keys[1], (N,), 0, 8) < 7).astype(jnp.int32), jax.random.fold_in(part_keys[1], 1), 0, 1),
        "ln_in_gain": jnp.clip(1.0 + 0.18 * jax.random.normal(keys[2], (C_Z,), jnp.float32), 0.1, 1.9),
        "ln_in_bias": bell_draw(keys[3], (C_Z,), 0.3, 1.5, (), jnp.float32),
        "w_edges": bell_draw(keys[4], (C_Z, 2 * C_HID), C_Z ** -0.5, 0.5),
        "w_edge_gates": bell_draw(keys[5], (C_Z, 2 * C_HID), C_Z ** -0.5, 0.5),
        "ln_out_gain": jnp.clip(1.0 + 0.18 * jax.random.normal(keys[6], (C_HID,), jnp.float32), 0.1, 1.9),
        "ln_out_bias": bell_draw(keys[7], (C_HID,), 0.3, 1.5, (), jnp.float32),
        "w_gate": bell_draw(keys[8], (C_Z, C_Z), C_Z ** -0.5, 0.5),
        "w_out": bell_draw(keys[9], (C_HID, C_Z), C_HID ** -0.5, 0.5),
    }


def layer_norm(values, gain, bias):
    mean = lax.optimization_barrier(jnp.mean(values, axis=-1, keepdims=True))
    centered = values - mean
    spread = lax.optimization_barrier(jnp.mean(centered * centered, axis=-1, keepdims=True))
    return centered * lax.rsqrt(spread + 1e-05) * gain + bias

def reference(pair, residue_mask, ln_in_gain, ln_in_bias, w_edges, w_edge_gates, ln_out_gain, ln_out_bias, w_gate, w_out):
    normed = layer_norm(pair.astype(jnp.float32), ln_in_gain, ln_in_bias).astype(jnp.bfloat16)
    normed_f = normed.astype(jnp.float32)
    proj = jnp.einsum('ijc,cd->ijd', normed_f, w_edges.astype(jnp.float32))
    gates = jnp.einsum('ijc,cd->ijd', normed_f, w_edge_gates.astype(jnp.float32))
    valid = residue_mask.astype(jnp.float32)
    pair_valid = valid[:, None, None] * valid[None, :, None]
    edges = (jax.nn.sigmoid(gates) * proj * pair_valid).astype(jnp.bfloat16)
    left = edges[:, :, :C_HID].astype(jnp.float32)
    right = edges[:, :, C_HID:].astype(jnp.float32)
    outer = jnp.einsum('ikc,jkc->ijc', left, right)
    outer_normed = layer_norm(outer, ln_out_gain, ln_out_bias).astype(jnp.bfloat16)
    gate = jax.nn.sigmoid(jnp.einsum('ijc,cd->ijd', normed_f, w_gate.astype(jnp.float32)))
    projected = jnp.einsum('ijc,cd->ijd', outer_normed.astype(jnp.float32), w_out.astype(jnp.float32))
    return (gate * projected).astype(jnp.bfloat16)
```

```python
import functools

import jax
import jax.numpy as jnp
from jax import lax
from jax.experimental import pallas as pl
from jax.experimental.pallas import tpu as pltpu
from jax.sharding import PartitionSpec as P

SQUARE = 8
PEERS = (2, 4, 6)
F32, BF16 = jnp.float32, jnp.bfloat16
VMEM = pl.BlockSpec(memory_space=pltpu.VMEM)
SMEM = pl.BlockSpec(memory_space=pltpu.SMEM)


def dot(a, b):
    return lax.dot_general(a, b, (((1,), (0,)), ((), ())), preferred_element_type=F32)


def row_means(values):
    lanes = values.shape[1]
    high = values.astype(BF16)
    low = (values - high.astype(F32)).astype(BF16)
    ones = jnp.full((2 * lanes, lanes), 1.0 / lanes, BF16)
    return dot(jnp.concatenate([high, low], axis=1), ones)


def sigmoid(x):
    return 0.5 + 0.5 * jnp.tanh(0.5 * x)


def layer_norm(values, mean, gain, bias):
    centered = values - mean
    spread = row_means(centered * centered)
    return (centered * lax.rsqrt(spread + 1e-05) * gain + bias).astype(BF16)


def input_norm(x, gain, bias):
    lanes = x.shape[1]
    mean = dot(x, jnp.full((lanes, lanes), 1.0 / lanes, BF16))
    return layer_norm(x.astype(F32), mean, gain, bias)


def gated(normed, w):
    half = w.shape[1] // 2
    both = dot(normed, w)
    return both[:, :half] * sigmoid(both[:, half:])


def k_valid(mask_ref, first, columns, lanes):
    at = lax.broadcasted_iota(jnp.int32, (columns, lanes), 0)
    out = jnp.zeros((columns, lanes), F32)
    for n in range(columns):
        out = jnp.where(at == n, mask_ref[first + n].astype(F32), out)
    return out


def right_edges(normed_ref, first, rows, w, valid):
    right = gated(normed_ref[pl.ds(first, rows), :], w)
    columns, lanes = valid.shape
    return (right.reshape(rows // columns, columns, lanes) * valid).reshape(rows, lanes)


def contract(lefts, right_ref, j_first, js, put, block, columns):
    at_once = 4
    chip_js = right_ref.shape[0] // len(lefts) // columns

    def step(g, carry):
        sums = [None] * at_once
        for s, (ref, first) in enumerate(lefts):
            for k in range(columns):
                left = ref[pl.ds(first + k, block, stride=columns), :]
                for n in range(at_once):
                    at = (s * chip_js + j_first + g * at_once + n) * columns + k
                    term = left * right_ref[pl.ds(at, 1), :]
                    sums[n] = term if sums[n] is None else sums[n] + term
        for n in range(at_once):
            put(g * at_once + n, sums[n])
        return carry

    lax.fori_loop(0, js // at_once, step, 0)


def split_weights(we_ref, wg_ref):
    half = we_ref.shape[1] // 2
    left = jnp.concatenate([we_ref[:, :half], wg_ref[:, :half]], axis=1)
    right = jnp.concatenate([we_ref[:, half:], wg_ref[:, half:]], axis=1)
    return left, right


def own_kernel(squares, block, columns, me_ref, mask_ref, pair_ref, gain_ref, bias_ref, we_ref, wg_ref, gate_ref, left_ref, right_ref, gates_ref, normed_ref):
    me = me_ref[0]
    lanes = pair_ref.shape[1]
    rows, js = block * columns, 2 * columns * columns
    w_left, w_right = split_weights(we_ref, wg_ref)
    valid = k_valid(mask_ref, me * columns, columns, lanes)
    for t in range(squares):
        x = pair_ref[pl.ds(pl.multiple_of(((me // SQUARE) ^ t) * rows, rows), rows), :]
        normed = input_norm(x, gain_ref[...], bias_ref[...])
        normed_ref[...] = normed
        left_ref[t * rows : (t + 1) * rows, :] = gated(normed, w_left)
        gates_ref[t * rows : (t + 1) * rows, :] = sigmoid(dot(normed, gate_ref[...]))
        first = pl.multiple_of(((me // 2) % (SQUARE // 2)) * js, js)
        right_ref[t * js : (t + 1) * js, :] = right_edges(normed_ref, first, js, w_right, valid)


def chunk_kernel(t, earlier, block, columns, *refs):
    me_ref, mask_ref, *refs = refs
    slabs, refs = refs[: len(PEERS)], refs[len(PEERS) :]
    own_left_ref, own_right_ref, gain_ref, bias_ref, we_ref, wg_ref, *refs = refs
    old_rights, refs = refs[: len(earlier)], refs[len(earlier) :]
    left_ref, right_ref, *refs = refs
    targets = list(earlier) + ([t] if t else [])
    outs, (normed_ref,) = refs[: 2 * len(targets)], refs[2 * len(targets) :]
    me = me_ref[0]
    lanes = left_ref.shape[1]
    rows, js = block * columns, 2 * columns * columns
    w_left, w_right = split_weights(we_ref, wg_ref)
    first = pl.multiple_of(((me // 2) % (SQUARE // 2)) * js, js)
    right_ref[:js, :] = own_right_ref[t * js : (t + 1) * js, :]
    for n, slab in enumerate(slabs):
        normed = input_norm(slab[...], gain_ref[...], bias_ref[...])
        normed_ref[n] = normed
        left_ref[n * rows : (n + 1) * rows, :] = gated(normed, w_left)
        valid = k_valid(mask_ref, (me ^ PEERS[n]) * columns, columns, lanes)
        right_ref[(n + 1) * js : (n + 2) * js, :] = right_edges(normed_ref.at[n], first, js, w_right, valid)
    lefts = [(own_left_ref, t * rows)] + [(left_ref, n * rows) for n in range(len(slabs))]
    rights = list(old_rights) + ([right_ref] if t else [])
    for n, right in enumerate(rights):
        both_cores(lefts, right, me % 2, outs[2 * n], outs[2 * n + 1], block, columns)


def both_cores(lefts, right, core, send_ref, keep_ref, block, columns):
    def put_send(j, value):
        send_ref[pl.ds(pl.multiple_of(j * block, block), block), :] = value.astype(BF16)

    def put_keep(j, value):
        keep_ref[pl.ds(pl.multiple_of(j * block, block), block), :] = value

    contract(lefts, right, (1 - core) * columns, columns, put_send, block, columns)
    contract(lefts, right, core * columns, columns, put_keep, block, columns)


def late_kernel(pairs, block, columns, *refs):
    n_left = 1 + max(p[1] for p in pairs)
    n_right = 1 + max(p[2] for p in pairs)
    me_ref, own_left_ref, *refs = refs
    lefts, refs = refs[:n_left], refs[n_left:]
    rights, outs = refs[:n_right], refs[n_right:]
    rows = block * columns
    for n, (t, a, b) in enumerate(pairs):
        slabs = [(own_left_ref, t * rows)] + [(lefts[a], m * rows) for m in range(len(PEERS))]
        both_cores(slabs, rights[b], me_ref[0] % 2, outs[2 * n], outs[2 * n + 1], block, columns)


def last_kernel(squares, block, columns, *refs):
    me_ref, mask_ref, mask_row_ref, *refs = refs
    each = squares + 1
    sums, refs = refs[: squares * each], refs[squares * each :]
    gates_ref, gain_ref, bias_ref, w_ref, out_ref, turned_ref = refs
    me = me_ref[0]
    rows = block * columns
    lanes = out_ref.shape[1]
    residues = mask_row_ref.shape[1]
    for t in range(squares):
        first = ((me // SQUARE) ^ t) * block
        at = lax.broadcasted_iota(jnp.int32, (block, residues), 0) + first
        chosen = jnp.where(lax.broadcasted_iota(jnp.int32, (block, residues), 1) == at, mask_row_ref[...], 0)
        valid = dot(chosen.astype(F32).astype(BF16), jnp.ones((residues, lanes), BF16))
        for j in range(columns):
            here = pl.ds(j * block, block)
            outer = sums[t * each][here, :]
            for other in sums[t * each + 1 : (t + 1) * each]:
                outer = outer + other[here, :].astype(F32)
            outer = outer * (valid * mask_ref[me * columns + j].astype(F32))
            normed = layer_norm(outer, row_means(outer), gain_ref[...], bias_ref[...])
            turned_ref[pl.ds(j, block, stride=columns), :] = dot(normed, w_ref[...])
        update = turned_ref[...] * gates_ref[t * rows : (t + 1) * rows, :]
        out_ref[pl.ds(pl.multiple_of(first * columns, rows), rows), :] = update.astype(BF16)


def call(kernel, operands, specs, outs, scratch=(), cost=1e6):
    return pl.pallas_call(
        kernel,
        out_shape=[jax.ShapeDtypeStruct(shape, dtype) for shape, dtype in outs],
        in_specs=specs,
        out_specs=[VMEM] * len(outs),
        scratch_shapes=list(scratch),
        cost_estimate=pl.CostEstimate(flops=int(cost), bytes_accessed=1 << 20, transcendentals=0),
        compiler_params=pltpu.CompilerParams(vmem_limit_bytes=32 << 20),
    )(*operands)


def local(size, pair, residue_mask, ln_in_gain, ln_in_bias, w_edges, w_edge_gates, ln_out_gain, ln_out_bias, w_gate, w_out):
    residues, columns, lanes = pair.shape
    squares = size // SQUARE
    block = residues // squares
    rows, js = block * columns, 2 * columns * columns
    index = lax.axis_index("row")
    me = index.astype(jnp.int32).reshape(1)
    square = index // SQUARE

    def swap(value, bits):
        return lax.ppermute(value, "row", [(i, i ^ bits) for i in range(size)])

    in_gain, in_bias = ln_in_gain.reshape(1, lanes), ln_in_bias.reshape(1, lanes)
    order = list(range(1, squares)) + [0]
    slabs = {}
    for t in order:
        own = lax.dynamic_slice_in_dim(pair, (square ^ t) * block, block, 0).reshape(rows, lanes)
        slabs[t] = [swap(own, bits) for bits in PEERS]

    with jax.named_scope("own_edges"):
        own_left, own_right, gates = call(
            functools.partial(own_kernel, squares, block, columns),
            (me, residue_mask, pair.reshape(residues * columns, lanes), in_gain, in_bias, w_edges, w_edge_gates, w_gate),
            [SMEM, SMEM] + [VMEM] * 6,
            [((squares * rows, lanes), F32), ((squares * js, lanes), F32), ((squares * rows, lanes), F32)],
            [pltpu.VMEM((rows, lanes), BF16)],
        )

    lefts, rights, parts, arrived = {}, {}, {}, {}

    def share(t, s, send, keep):
        other = swap(send, 1)
        if s == 0:
            parts[t, 0] = [keep, other]
        else:
            arrived[t ^ s, s] = swap((keep + other.astype(F32)).astype(BF16), SQUARE * s)

    piece = [((rows, lanes), BF16), ((rows, lanes), F32)]
    done = set()
    for t in order:
        earlier = tuple(s for s in rights if s)
        targets = earlier + ((t,) if t else ())
        with jax.named_scope("chunk"):
            lefts[t], rights[t], *made = call(
                functools.partial(chunk_kernel, t, earlier, block, columns),
                (me, residue_mask, *slabs[t], own_left, own_right, in_gain, in_bias, w_edges, w_edge_gates, *(rights[s] for s in earlier)),
                [SMEM, SMEM] + [VMEM] * (len(PEERS) + 6 + len(earlier)),
                [((len(PEERS) * rows, lanes), F32), ((SQUARE // 2 * js, lanes), F32)] + piece * len(targets),
                [pltpu.VMEM((len(PEERS), rows, lanes), BF16)],
            )
        for n, s in enumerate(targets):
            share(t, s, made[2 * n], made[2 * n + 1])
            done.add((t, s))
    left_over = [(t, s) for s in order for t in order if (t, s) not in done]
    with jax.named_scope("own_outer"):
        made = call(
            functools.partial(late_kernel, [(t, order.index(t), order.index(s)) for t, s in left_over], block, columns),
            (me, own_left, *(lefts[t] for t in order), *(rights[t] for t in order)),
            [SMEM] + [VMEM] * (1 + 2 * squares),
            piece * len(left_over),
        )
    for n, (t, s) in enumerate(left_over):
        share(t, s, made[2 * n], made[2 * n + 1])

    with jax.named_scope("update"):
        sums = []
        for t in range(squares):
            sums += parts[t, 0] + [arrived[t, s] for s in range(1, squares)]
        (update,) = call(
            functools.partial(last_kernel, squares, block, columns),
            (me, residue_mask, residue_mask.reshape(1, residues), *sums, gates, ln_out_gain.reshape(1, lanes), ln_out_bias.reshape(1, lanes), w_out),
            [SMEM, SMEM] + [VMEM] * (5 + len(sums)),
            [((residues * columns, lanes), BF16)],
            [pltpu.VMEM((rows, lanes), F32)],
        )
    return update.reshape(residues, columns, lanes)


def solution(mesh):
    return jax.shard_map(
        functools.partial(local, mesh.shape["row"]),
        mesh=mesh,
        in_specs=(P("groups", "row", None), P("groups"), P(), P(), P(), P(), P(), P(), P(), P()),
        out_specs=P("groups", "row", None),
        check_vma=False,
    )
```

```python
import functools

import jax
import jax.numpy as jnp
from jax import lax
from jax.experimental import pallas as pl
from jax.experimental.pallas import tpu as pltpu
from jax.sharding import PartitionSpec as P

SQUARE = 8
CORE, Y, Z, CORNER = 1, 2, 4, 6
FAR = (Y, Y + CORE, Z, Z + CORE, CORNER, CORNER + CORE)
F32, BF16 = jnp.float32, jnp.bfloat16

VMEM = pl.BlockSpec(memory_space=pltpu.VMEM)
SMEM = pl.BlockSpec(memory_space=pltpu.SMEM)


def dot(a, b):
    return lax.dot_general(a, b, (((1,), (0,)), ((), ())), preferred_element_type=F32)


def lane_means(x):
    lanes = x.shape[1]
    return dot(x, jnp.full((lanes, lanes), 1.0 / lanes, BF16))


def two_part_means(values):
    lanes = values.shape[1]
    high = values.astype(BF16)
    low = (values - high.astype(F32)).astype(BF16)
    ones = jnp.full((2 * lanes, lanes), 1.0 / lanes, BF16)
    return dot(jnp.concatenate([high, low], axis=1), ones)


def sigmoid(x):
    return 0.5 + 0.5 * jnp.tanh(0.5 * x)


def layer_norm(values, mean, gain, bias):
    centered = values - mean
    spread = lane_means((centered * centered).astype(BF16))
    return (centered * lax.rsqrt(spread + 1e-05) * gain + bias).astype(BF16)


def input_norm(x, gain, bias):
    return layer_norm(x.astype(F32), lane_means(x), gain, bias)


def gated(normed, w):
    half = w.shape[1] // 2
    both = dot(normed, w)
    return both[:, :half] * sigmoid(both[:, half:])


def k_valid(mask_ref, first, columns, lanes):
    at = lax.broadcasted_iota(jnp.int32, (columns, lanes), 0)
    out = jnp.zeros((columns, lanes), F32)
    for n in range(columns):
        out = jnp.where(at == n, mask_ref[first + n].astype(F32), out)
    return out


def split_weights(we_ref, wg_ref):
    half = we_ref.shape[1] // 2
    left = jnp.concatenate([we_ref[:, :half], wg_ref[:, :half]], axis=1)
    right = jnp.concatenate([we_ref[:, half:], wg_ref[:, half:]], axis=1)
    return left, right


def right_edges(normed_ref, first, rows, w, valid):
    right = gated(normed_ref[pl.ds(first, rows), :], w)
    columns, lanes = valid.shape
    return (right.reshape(rows // columns, columns, lanes) * valid).reshape(rows, lanes)


def contract(slabs, start, out, block, columns):
    at_once = 4

    def rows_of(j):
        return pl.ds(pl.multiple_of(j * block, block), block)

    def step(g, carry):
        js = [g * at_once + n for n in range(at_once)]
        sums = [None if start is None else start[rows_of(j), :] for j in js]
        for left_ref, right_ref in slabs:
            for k in range(columns):
                left = left_ref[pl.ds(k, block, stride=columns), :]
                for n, j in enumerate(js):
                    term = left * right_ref[pl.ds(j * columns + k, 1), :]
                    sums[n] = term if sums[n] is None else sums[n] + term
        for n, j in enumerate(js):
            out[rows_of(j), :] = sums[n].astype(out.dtype)
        return carry

    lax.fori_loop(0, columns // at_once, step, 0)


def block_rows(me, t, rows):
    return pl.ds(pl.multiple_of(((me // SQUARE) ^ t) * rows, rows), rows)


def edges_of(raws, lefts, rights, valids, gain, bias, weights, normed_ref, me, js, more=None):
    w_left, w_right = weights
    for m, x in enumerate(raws):
        normed = input_norm(x, gain, bias)
        normed_ref[m] = normed
        lefts[m][...] = gated(normed, w_left)
        if more is not None:
            more(m, normed)
    for m in range(len(raws)):
        first = pl.multiple_of((me % SQUARE) * js, js)
        rights[m][...] = right_edges(normed_ref.at[m], first, js, w_right, valids[m])


def own_kernel(squares, block, columns, *refs):
    me_ref, mask_ref, mask_row_ref, *refs = refs
    slabs, refs = refs[:2], refs[2:]
    gain_ref, bias_ref, we_ref, wg_ref, gate_ref, w_out_ref, out_gain_ref, out_bias_ref, *refs = refs
    gates_ref, far_valid_ref, i_valid_ref, j_valid_ref, w_copy_ref, norm_copy_ref, *refs = refs
    lefts, refs = refs[: 2 * squares], refs[2 * squares :]
    rights, refs = refs[: 2 * squares], refs[2 * squares :]
    shares, (normed_ref,) = refs[:-1], refs[-1:]
    me = me_ref[0]
    lanes = gates_ref.shape[1]
    rows, js = block * columns, columns * columns
    residues = mask_row_ref.shape[1]
    valids = [k_valid(mask_ref, (me ^ b) * columns, columns, lanes) for b in (0, CORE)]

    def gates(m, normed):
        if m < squares:
            gates_ref[m * rows : (m + 1) * rows, :] = sigmoid(dot(normed, gate_ref[...]))

    edges_of(
        [slab[block_rows(me, t, rows), :] for slab in slabs for t in range(squares)],
        lefts, rights, [valids[0]] * squares + [valids[1]] * squares,
        gain_ref[...], bias_ref[...], split_weights(we_ref, wg_ref), normed_ref, me, js, gates,
    )
    for t in range(squares):
        for s in range(1, squares):
            terms = [(lefts[t], rights[s]), (lefts[squares + t], rights[squares + s])]
            contract(terms, None, shares[t * (squares - 1) + s - 1], block, columns)
    for n, bits in enumerate(FAR):
        far_valid_ref[n * columns : (n + 1) * columns, :] = k_valid(mask_ref, (me ^ bits) * columns, columns, lanes)
    j_valid_ref[...] = valids[0]
    for t in range(squares):
        at = lax.broadcasted_iota(jnp.int32, (block, residues), 0) + ((me // SQUARE) ^ t) * block
        chosen = jnp.where(lax.broadcasted_iota(jnp.int32, (block, residues), 1) == at, mask_row_ref[...], 0)
        i_valid_ref[t * block : (t + 1) * block, :] = dot(chosen.astype(F32).astype(BF16), jnp.ones((residues, lanes), BF16))
    w_copy_ref[...] = w_out_ref[...]
    norm_copy_ref[:1, :] = out_gain_ref[...]
    norm_copy_ref[1:, :] = out_bias_ref[...]


def piece_kernel(new, old, products, block, columns, *refs):
    refs = list(refs)

    def take(n):
        out = refs[:n]
        del refs[:n]
        return out

    rows, js = block * columns, columns * columns
    if new:
        me = take(1)[0][0]
        raw = take(len(new))
        valid_ref, gain_ref, bias_ref, we_ref, wg_ref = take(5)
    old_lefts, old_rights = take(len(old)), take(len(old))
    starts = [take(1)[0] if begun else None for _, _, begun in products]
    new_lefts, new_rights = take(len(new)), take(len(new))
    outs = take(len(products))
    edges = dict(zip(old, zip(old_lefts, old_rights)))
    if new:
        edges_of(
            [x[block_rows(me, t, rows) if x.shape[0] > rows else pl.ds(0, rows), :] for x, (_, t) in zip(raw, new)],
            new_lefts, new_rights, [valid_ref[pl.ds(FAR.index(b) * columns, columns), :] for b, _ in new],
            gain_ref[...], bias_ref[...], split_weights(we_ref, wg_ref), refs[0], me, js,
        )
        edges.update(zip(new, zip(new_lefts, new_rights)))
    for ((t, s), slabs, _), start, out in zip(products, starts, outs):
        contract([(edges[b, t][0], edges[b, s][1]) for b in slabs], start, out, block, columns)


def last_kernel(t, n_sums, block, columns, me_ref, *refs):
    i_valid_ref, j_valid_ref, *refs = refs
    sums, refs = refs[:n_sums], refs[n_sums:]
    gates_ref, norm_ref, w_ref, *refs = refs
    out_ref, turned_ref = refs[-2:]
    rows = block * columns
    outer = sums[0][...]
    for other in sums[1:]:
        outer = outer + other[...].astype(F32)
    i_valid = i_valid_ref[t * block : (t + 1) * block, :]
    outer = outer * jnp.concatenate([i_valid * j_valid_ref[j : j + 1, :] for j in range(columns)], axis=0)
    normed = layer_norm(outer, two_part_means(outer), norm_ref[:1, :], norm_ref[1:, :])
    projected = dot(normed, w_ref[...])
    for j in range(columns):
        turned_ref[pl.ds(j, block, stride=columns), :] = projected[j * block : (j + 1) * block, :]
    out_ref[...] = (turned_ref[...] * gates_ref[t * rows : (t + 1) * rows, :]).astype(BF16)


def call(kernel, operands, smem, outs, scratch=()):
    return pl.pallas_call(
        kernel,
        out_shape=[jax.ShapeDtypeStruct(shape, dtype) for shape, dtype in outs],
        in_specs=[SMEM] * smem + [VMEM] * (len(operands) - smem),
        out_specs=[VMEM] * len(outs),
        scratch_shapes=list(scratch),
        compiler_params=pltpu.CompilerParams(vmem_limit_bytes=12 << 20),
    )(*operands)


def local(size, pair, residue_mask, ln_in_gain, ln_in_bias, w_edges, w_edge_gates, ln_out_gain, ln_out_bias, w_gate, w_out):
    residues, columns, lanes = pair.shape
    squares = size // SQUARE
    block = residues // squares
    rows, js = block * columns, columns * columns
    index = lax.axis_index("row")
    me = index.astype(jnp.int32).reshape(1)
    square = index // SQUARE

    def swap(value, bits):
        return lax.ppermute(value, "row", [(i, i ^ bits) for i in range(size)])

    in_gain, in_bias = ln_in_gain.reshape(1, lanes), ln_in_bias.reshape(1, lanes)
    flat = pair.reshape(residues * columns, lanes)
    order = list(range(1, squares)) + [0]
    raw = {}
    whole = swap(flat, CORNER)
    for t in order:
        own = lax.dynamic_slice_in_dim(pair, (square ^ t) * block, block, 0).reshape(rows, lanes)
        for b in (Z, Y):
            raw[b, t] = swap(own, b)
    near_whole = swap(flat, CORE)

    tile = lambda n, dtype=F32: ((n, lanes), dtype)
    with jax.named_scope("own_slab"):
        gates, far_valid, i_valid, j_valid, w_last, norm_last, *made = call(
            functools.partial(own_kernel, squares, block, columns),
            (me, residue_mask, residue_mask.reshape(1, residues), flat, near_whole, in_gain, in_bias, w_edges, w_edge_gates)
            + (w_gate, w_out, ln_out_gain.reshape(1, lanes), ln_out_bias.reshape(1, lanes)),
            2,
            [tile(squares * rows), tile(len(FAR) * columns), tile(squares * block), tile(columns), tile(lanes, BF16), tile(2)]
            + [tile(rows)] * (2 * squares) + [tile(js)] * (2 * squares) + [tile(rows)] * (squares * (squares - 1)),
            [pltpu.VMEM((2 * squares, rows, lanes), BF16)],
        )
    near = [(b, t) for b in (0, CORE) for t in range(squares)]
    lefts = dict(zip(near, made))
    rights = dict(zip(near, made[2 * squares :]))
    others = [(t, s) for t in range(squares) for s in range(1, squares)]
    sums = dict(zip(others, made[4 * squares :]))

    def pieces(new, products):
        read = sorted({(b, u) for (t, s), slabs, *_ in products for b in slabs for u in (t, s)} - set(new))
        operands = []
        if new:
            operands += [me] + [raw[p] for p in new] + [far_valid, in_gain, in_bias, w_edges, w_edge_gates]
        operands += [lefts[p] for p in read] + [rights[p] for p in read] + [sums[ts] for ts, _, begun, _ in products if begun]
        made = call(
            functools.partial(piece_kernel, tuple(new), tuple(read), tuple(p[:3] for p in products), block, columns),
            operands,
            1 if new else 0,
            [tile(rows)] * len(new) + [tile(js)] * len(new) + [tile(rows, dtype) for *_, dtype in products],
            [pltpu.VMEM((len(new), rows, lanes), BF16)] if new else [],
        )
        for n, p in enumerate(new):
            lefts[p], rights[p] = made[n], made[len(new) + n]
        return made[2 * len(new) :]

    def hand_on(names, after):
        for b, ts in names:
            value, _ = lax.optimization_barrier((raw[b, ts[0]], after))
            value = swap(value, CORE)
            raw.update({(b + CORE, t): value for t in ts})

    first, rest = order[0], order[1:]
    raw.update({(CORNER, t): whole for t in order})
    missing = {ts: set(FAR) for ts in others}
    arrived = {}

    def work(step):
        have = set(lefts) | set(step)
        products = []
        for (t, s), slabs in missing.items():
            now = tuple(b for b in FAR if b in slabs and (b, t) in have and (b, s) in have)
            if now:
                slabs -= set(now)
                products.append(((t, s), now, True, F32 if slabs else BF16))
        with jax.named_scope("pieces"):
            made = pieces(step, products)
        for ((t, s), *_, dtype), value in zip(products, made):
            if dtype == F32:
                sums[t, s] = value
            else:
                arrived[t ^ s, s] = swap(value, SQUARE * s)
        return lefts[step[0]]

    hand_on([(Z, [first])], gates)
    after = work([(Z, first)])
    hand_on([(Y, [first]), (CORNER, order)], after)
    after = work([(Y, first), (CORNER, first), (Z + CORE, first)])
    for t in rest:
        hand_on([(Z, [t]), (Y, [t])], after)
    work([(Y + CORE, first), (CORNER + CORE, first)])
    for t in rest:
        work([(b, t) for b in FAR])
    with jax.named_scope("own_outer"):
        own_sums = pieces([], [((t, 0), (0, CORE, *FAR), False, F32) for t in range(squares)])

    update = None
    for t in range(squares):
        others = [arrived[t, s] for s in range(1, squares)]
        before = () if update is None else (update,)
        operands = (me, i_valid, j_valid, own_sums[t], *others, gates, norm_last, w_last, *before)
        with jax.named_scope("update"):
            update = pl.pallas_call(
                functools.partial(last_kernel, t, 1 + len(others), block, columns),
                out_shape=jax.ShapeDtypeStruct((residues * columns, lanes), BF16),
                grid_spec=pltpu.PrefetchScalarGridSpec(
                    num_scalar_prefetch=1,
                    grid=(1,),
                    in_specs=[VMEM] * (6 + len(others)) + [pl.BlockSpec(memory_space=pl.ANY)] * len(before),
                    out_specs=pl.BlockSpec((rows, lanes), lambda i, me_ref, t=t: ((me_ref[0] // SQUARE) ^ t, 0)),
                    scratch_shapes=[pltpu.VMEM((rows, lanes), F32)],
                ),
                input_output_aliases={len(operands) - 1: 0} if before else {},
                compiler_params=pltpu.CompilerParams(vmem_limit_bytes=12 << 20),
            )(*operands)
    return update.reshape(residues, columns, lanes)


def solution(mesh):
    return jax.shard_map(
        functools.partial(local, mesh.shape["row"]),
        mesh=mesh,
        in_specs=(P("groups", "row", None), P("groups"), P(), P(), P(), P(), P(), P(), P(), P()),
        out_specs=P("groups", "row", None),
        check_vma=False,
    )
```

```python
import functools

import jax
import jax.numpy as jnp
from jax import lax
from jax.experimental import pallas as pl
from jax.experimental.pallas import tpu as pltpu
from jax.sharding import PartitionSpec as P

SQUARE = 8
CORE, Y, Z, CORNER = 1, 2, 4, 6
FAR = (Y, Y + CORE, Z, Z + CORE, CORNER, CORNER + CORE)
F32, BF16 = jnp.float32, jnp.bfloat16

VMEM = pl.BlockSpec(memory_space=pltpu.VMEM)
SMEM = pl.BlockSpec(memory_space=pltpu.SMEM)


def dot(a, b):
    return lax.dot_general(a, b, (((1,), (0,)), ((), ())), preferred_element_type=F32)


def lane_means(x):
    lanes = x.shape[1]
    return dot(x, jnp.full((lanes, lanes), 1.0 / lanes, BF16))


def two_part_means(values):
    lanes = values.shape[1]
    high = values.astype(BF16)
    low = (values - high.astype(F32)).astype(BF16)
    ones = jnp.full((2 * lanes, lanes), 1.0 / lanes, BF16)
    return dot(jnp.concatenate([high, low], axis=1), ones)


def centred(x):
    lanes = x.shape[1]
    eye = lax.broadcasted_iota(jnp.int32, (lanes, lanes), 0) == lax.broadcasted_iota(jnp.int32, (lanes, lanes), 1)
    return dot(x, (jnp.where(eye, 1.0, 0.0) - 1.0 / lanes).astype(BF16))


def normalised(centered, gain, bias):
    spread = lane_means((centered * centered).astype(BF16))
    return (centered * lax.rsqrt(spread + 1e-05) * gain + bias).astype(BF16)


def gated(normed, weights):
    half_p = dot(normed, weights[0])
    return half_p + half_p * jnp.tanh(dot(normed, weights[1]))


def halved(w):
    return (w.astype(F32) * 0.5).astype(BF16)


def k_valid(mask_ref, first, columns, lanes):
    at = lax.broadcasted_iota(jnp.int32, (columns, lanes), 0)
    out = jnp.zeros((columns, lanes), F32)
    for n in range(columns):
        out = jnp.where(at == n, mask_ref[first + n].astype(F32), out)
    return out


def split_weights(we_ref, wg_ref):
    half = we_ref.shape[1] // 2
    left = halved(we_ref[:, :half]), halved(wg_ref[:, :half])
    right = halved(we_ref[:, half:]), halved(wg_ref[:, half:])
    return left, right


def contract(slabs, start, out, block, columns):
    at_once = min(32, block)
    for i in range(0, block, at_once):
        here = [pl.ds(j * block + i, at_once) for j in range(columns)]
        sums = [None if start is None else start[rows, :] for rows in here]
        for left_ref, right_ref in slabs:
            for k in range(columns):
                left = left_ref[pl.ds(i * columns + k, at_once, stride=columns), :]
                for j in range(columns):
                    term = left * right_ref[pl.ds(j * columns + k, 1), :]
                    sums[j] = term if sums[j] is None else sums[j] + term
        for rows, value in zip(here, sums):
            out[rows, :] = value.astype(out.dtype)


def block_rows(me, t, rows):
    return pl.ds(pl.multiple_of(((me // SQUARE) ^ t) * rows, rows), rows)


def right_edges(normed, weights, valids, refs):
    right = gated(normed, weights)
    columns, lanes = valids[0].shape
    js = normed.shape[0] // len(refs)
    for m, (valid, ref) in enumerate(zip(valids, refs)):
        ref[...] = (right[m * js : (m + 1) * js, :].reshape(columns, columns, lanes) * valid).reshape(js, lanes)


def place_rows(me, js):
    return pl.ds(pl.multiple_of((me % SQUARE) * js, js), js)


def edges_of(raws, lefts, rights, valids, gain, bias, weights, normed_ref, me, js):
    w_left, w_right = weights
    for m, x in enumerate(raws):
        normed_ref[m] = normalised(centred(x), gain, bias)
    for m in range(len(raws)):
        lefts[m][...] = gated(normed_ref[m], w_left)
    wanted = [m for m in range(len(raws)) if rights[m] is not None]
    if wanted:
        normed = jnp.concatenate([normed_ref[m, place_rows(me, js), :] for m in wanted], axis=0)
        right_edges(normed, w_right, [valids[m] for m in wanted], [rights[m] for m in wanted])


def own_kernel(squares, block, columns, *refs):
    me_ref, mask_ref, mask_row_ref, *refs = refs
    slabs, refs = refs[:2], refs[2:]
    gain_ref, bias_ref, we_ref, wg_ref, gate_ref, w_out_ref, out_gain_ref, out_bias_ref, *refs = refs
    gates_ref, far_valid_ref, i_valid_ref, j_valid_ref, w_copy_ref, norm_copy_ref, *refs = refs
    lefts, refs = refs[: 2 * squares], refs[2 * squares :]
    rights, refs = refs[: 2 * squares], refs[2 * squares :]
    shares, (normed_ref,) = refs[:-1], refs[-1:]
    me = me_ref[0]
    lanes = gates_ref.shape[1]
    rows, js = block * columns, columns * columns
    residues = mask_row_ref.shape[1]
    valids = [k_valid(mask_ref, (me ^ b) * columns, columns, lanes) for b in (0, CORE)]

    edges_of(
        [slab[block_rows(me, t, rows), :] for slab in slabs for t in range(squares)],
        lefts, rights, [valids[0]] * squares + [valids[1]] * squares,
        gain_ref[...], bias_ref[...], split_weights(we_ref, wg_ref), normed_ref, me, js,
    )
    half_gate = halved(gate_ref[...])
    for t in range(squares):
        gates_ref[t * rows : (t + 1) * rows, :] = 0.5 + 0.5 * jnp.tanh(dot(normed_ref[t], half_gate))
    for t in range(squares):
        for s in range(1, squares):
            terms = [(lefts[t], rights[s]), (lefts[squares + t], rights[squares + s])]
            contract(terms, None, shares[t * (squares - 1) + s - 1], block, columns)
    for n, bits in enumerate(FAR):
        far_valid_ref[n * columns : (n + 1) * columns, :] = k_valid(mask_ref, (me ^ bits) * columns, columns, lanes)
    j_valid_ref[...] = valids[0]
    for t in range(squares):
        at = lax.broadcasted_iota(jnp.int32, (block, residues), 0) + ((me // SQUARE) ^ t) * block
        chosen = jnp.where(lax.broadcasted_iota(jnp.int32, (block, residues), 1) == at, mask_row_ref[...], 0)
        i_valid_ref[t * block : (t + 1) * block, :] = dot(chosen.astype(F32).astype(BF16), jnp.ones((residues, lanes), BF16))
    w_copy_ref[...] = w_out_ref[...]
    norm_copy_ref[:1, :] = out_gain_ref[...]
    norm_copy_ref[1:, :] = out_bias_ref[...]


def piece_kernel(new, old, products, block, columns, *refs):
    refs = list(refs)

    def take(n):
        out = refs[:n]
        del refs[:n]
        return out

    rows, js = block * columns, columns * columns
    late = [p for p in old if p[1] == 0 and p[0] in FAR] if not new else []
    me = take(1)[0][0]
    raw = take(len(new) + len(late))
    valid_ref, gain_ref, bias_ref, we_ref, wg_ref = take(5)
    old_lefts, old_rights = take(len(old)), take(len(old) - len(late))
    starts = [take(1)[0] if begun else None for _, _, begun in products]
    made = [p for p in new if p[1]]
    new_lefts, new_rights = take(len(new)), take(len(made))
    outs = take(len(products))
    lefts = dict(zip(old, old_lefts))
    rights = dict(zip([p for p in old if p not in late], old_rights))
    weights = split_weights(we_ref, wg_ref)
    valid = lambda b: valid_ref[pl.ds(FAR.index(b) * columns, columns), :]
    if new:
        lefts.update(zip(new, new_lefts))
        rights.update(zip(made, new_rights))
        edges_of(
            [x[block_rows(me, t, rows) if x.shape[0] > rows else pl.ds(0, rows), :] for x, (_, t) in zip(raw, new)],
            new_lefts, [rights.get(p) for p in new], [valid(b) for b, _ in new],
            gain_ref[...], bias_ref[...], weights, refs[0], me, js,
        )
    if late:
        at = (me // SQUARE) * rows + (me % SQUARE) * js
        x = [x[pl.ds(pl.multiple_of(at, js), js) if x.shape[0] > rows else place_rows(me, js), :] for x in raw]
        normed = normalised(centred(jnp.concatenate(x, axis=0)), gain_ref[...], bias_ref[...])
        rights.update({p: refs[0].at[m] for m, p in enumerate(late)})
        right_edges(normed, weights[1], [valid(b) for b, _ in late], [rights[p] for p in late])
    for ((t, s), slabs, _), start, out in zip(products, starts, outs):
        contract([(lefts[b, t], rights[b, s]) for b in slabs], start, out, block, columns)


def last_kernel(t, n_sums, block, columns, me_ref, *refs):
    i_valid_ref, j_valid_ref, *refs = refs
    sums, refs = refs[:n_sums], refs[n_sums:]
    gates_ref, norm_ref, w_ref, *refs = refs
    out_ref, turned_ref = refs[-2:]
    rows = block * columns
    outer = sums[0][...]
    for other in sums[1:]:
        outer = outer + other[...].astype(F32)
    i_valid = i_valid_ref[t * block : (t + 1) * block, :]
    outer = outer * jnp.concatenate([i_valid * j_valid_ref[j : j + 1, :] for j in range(columns)], axis=0)
    normed = normalised(outer - two_part_means(outer), norm_ref[:1, :], norm_ref[1:, :])
    projected = dot(normed, w_ref[...])
    for j in range(columns):
        turned_ref[pl.ds(j, block, stride=columns), :] = projected[j * block : (j + 1) * block, :]
    out_ref[...] = (turned_ref[...] * gates_ref[t * rows : (t + 1) * rows, :]).astype(BF16)


def call(kernel, operands, smem, outs, scratch=()):
    return pl.pallas_call(
        kernel,
        out_shape=[jax.ShapeDtypeStruct(shape, dtype) for shape, dtype in outs],
        in_specs=[SMEM] * smem + [VMEM] * (len(operands) - smem),
        out_specs=[VMEM] * len(outs),
        scratch_shapes=list(scratch),
        compiler_params=pltpu.CompilerParams(vmem_limit_bytes=12 << 20),
    )(*operands)


def local(size, pair, residue_mask, ln_in_gain, ln_in_bias, w_edges, w_edge_gates, ln_out_gain, ln_out_bias, w_gate, w_out):
    residues, columns, lanes = pair.shape
    squares = size // SQUARE
    block = residues // squares
    rows, js = block * columns, columns * columns
    index = lax.axis_index("row")
    me = index.astype(jnp.int32).reshape(1)
    square = index // SQUARE

    def swap(value, bits):
        return lax.ppermute(value, "row", [(i, i ^ bits) for i in range(size)])

    in_gain, in_bias = ln_in_gain.reshape(1, lanes), ln_in_bias.reshape(1, lanes)
    flat = pair.reshape(residues * columns, lanes)
    order = list(range(1, squares)) + [0]
    raw = {}
    own = {t: lax.dynamic_slice_in_dim(pair, (square ^ t) * block, block, 0).reshape(rows, lanes) for t in order}

    def fetch(names, after=()):
        for b, t in names:
            raw[b, t] = swap(lax.optimization_barrier((own[t], after))[0] if len(after) else own[t], b)

    whole = swap(flat, CORNER)
    raw.update({(CORNER, t): whole for t in order})
    for t in order:
        fetch([(b, t) for b in (Z, Y)])
    near_whole = swap(flat, CORE)

    tile = lambda n, dtype=F32: ((n, lanes), dtype)
    with jax.named_scope("own_slab"):
        gates, far_valid, i_valid, j_valid, w_last, norm_last, *made = call(
            functools.partial(own_kernel, squares, block, columns),
            (me, residue_mask, residue_mask.reshape(1, residues), flat, near_whole, in_gain, in_bias, w_edges, w_edge_gates)
            + (w_gate, w_out, ln_out_gain.reshape(1, lanes), ln_out_bias.reshape(1, lanes)),
            2,
            [tile(squares * rows), tile(len(FAR) * columns), tile(squares * block), tile(columns), tile(lanes, BF16), tile(2)]
            + [tile(rows)] * (2 * squares) + [tile(js)] * (2 * squares) + [tile(rows)] * (squares * (squares - 1)),
            [pltpu.VMEM((2 * squares, rows, lanes), BF16)],
        )
    near = [(b, t) for b in (0, CORE) for t in range(squares)]
    lefts = dict(zip(near, made))
    rights = dict(zip(near, made[2 * squares :]))
    others = [(t, s) for t in range(squares) for s in range(1, squares)]
    sums = dict(zip(others, made[4 * squares :]))

    def pieces(new, products):
        read = sorted({(b, u) for (t, s), slabs, *_ in products for b in slabs for u in (t, s)} - set(new))
        late = [p for p in read if p not in rights]
        made = [p for p in new if p[1]]
        operands = [me] + [raw[p] for p in (*new, *late)] + [far_valid, in_gain, in_bias, w_edges, w_edge_gates]
        operands += [lefts[p] for p in read] + [rights[p] for p in read if p in rights]
        operands += [sums[ts] for ts, _, begun, _ in products if begun]
        scratch = pltpu.VMEM((len(new), rows, lanes), BF16) if new else pltpu.VMEM((len(late), js, lanes), F32)
        out = call(
            functools.partial(piece_kernel, tuple(new), tuple(read), tuple(p[:3] for p in products), block, columns),
            operands,
            1,
            [tile(rows)] * len(new) + [tile(js)] * len(made) + [tile(rows, dtype) for *_, dtype in products],
            [scratch],
        )
        lefts.update(zip(new, out))
        rights.update(zip(made, out[len(new) :]))
        return out[len(new) + len(made) :]

    def hand_on(names, after):
        for b, t in names:
            raw[b + CORE, t] = swap(lax.optimization_barrier((raw[b, t], after))[0], CORE)

    first, rest = order[0], order[1:]
    missing = {ts: set(FAR) for ts in others}
    arrived = {}

    def work(step):
        have = set(lefts) | set(step)
        products = []
        for (t, s), slabs in missing.items():
            now = tuple(b for b in FAR if b in slabs and (b, t) in have and (b, s) in have)
            if now:
                slabs -= set(now)
                products.append(((t, s), now, True, F32 if slabs else BF16))
        with jax.named_scope("pieces"):
            made = pieces(step, products)
        for ((t, s), *_, dtype), value in zip(products, made):
            if dtype == F32:
                sums[t, s] = value
            else:
                arrived[t ^ s, s] = swap(value, SQUARE * s)
        return lefts[step[-1]]

    hand_on([(Z, first), (Y, first)], gates)
    whole_of_core = swap(lax.optimization_barrier((whole, gates))[0], CORE)
    raw.update({(CORNER + CORE, t): whole_of_core for t in order})
    after = work([(Z, first), (Y, first), (CORNER, first)])
    for t in rest:
        hand_on([(b, t) for b in (Z, Y)], after)
    work([(b + CORE, first) for b in (Z, Y, CORNER)])
    for t in rest:
        work([(b, t) for b in FAR])
    with jax.named_scope("own_outer"):
        own_sums = pieces([], [((t, 0), (0, CORE, *FAR), False, F32) for t in range(squares)])

    update = None
    for t in range(squares):
        others = [arrived[t, s] for s in range(1, squares)]
        before = () if update is None else (update,)
        operands = (me, i_valid, j_valid, own_sums[t], *others, gates, norm_last, w_last, *before)
        with jax.named_scope("update"):
            update = pl.pallas_call(
                functools.partial(last_kernel, t, 1 + len(others), block, columns),
                out_shape=jax.ShapeDtypeStruct((residues * columns, lanes), BF16),
                grid_spec=pltpu.PrefetchScalarGridSpec(
                    num_scalar_prefetch=1,
                    grid=(1,),
                    in_specs=[VMEM] * (6 + len(others)) + [pl.BlockSpec(memory_space=pl.ANY)] * len(before),
                    out_specs=pl.BlockSpec((rows, lanes), lambda i, me_ref, t=t: ((me_ref[0] // SQUARE) ^ t, 0)),
                    scratch_shapes=[pltpu.VMEM((rows, lanes), F32)],
                ),
                input_output_aliases={len(operands) - 1: 0} if before else {},
                compiler_params=pltpu.CompilerParams(vmem_limit_bytes=12 << 20),
            )(*operands)
    return update.reshape(residues, columns, lanes)


def solution(mesh):
    return jax.shard_map(
        functools.partial(local, mesh.shape["row"]),
        mesh=mesh,
        in_specs=(P("groups", "row", None), P("groups"), P(), P(), P(), P(), P(), P(), P(), P()),
        out_specs=P("groups", "row", None),
        check_vma=False,
    )
```

```python
import functools

import jax
import jax.numpy as jnp
from jax import lax
from jax.experimental import pallas as pl
from jax.experimental.pallas import tpu as pltpu
from jax.sharding import PartitionSpec as P

SQUARE = 8
CORE, Y, Z, CORNER = 1, 2, 4, 6
FAR = (Y, Y + CORE, Z, Z + CORE, CORNER, CORNER + CORE)
F32, BF16 = jnp.float32, jnp.bfloat16

VMEM = pl.BlockSpec(memory_space=pltpu.VMEM)
SMEM = pl.BlockSpec(memory_space=pltpu.SMEM)


def dot(a, b):
    return lax.dot_general(a, b, (((1,), (0,)), ((), ())), preferred_element_type=F32)


def lane_means(x):
    lanes = x.shape[1]
    return dot(x, jnp.full((lanes, lanes), 1.0 / lanes, BF16))


def two_part_means(values):
    lanes = values.shape[1]
    high = values.astype(BF16)
    low = (values - high.astype(F32)).astype(BF16)
    ones = jnp.full((2 * lanes, lanes), 1.0 / lanes, BF16)
    return dot(jnp.concatenate([high, low], axis=1), ones)


def centred(x):
    lanes = x.shape[1]
    eye = lax.broadcasted_iota(jnp.int32, (lanes, lanes), 0) == lax.broadcasted_iota(jnp.int32, (lanes, lanes), 1)
    return dot(x, (jnp.where(eye, 1.0, 0.0) - 1.0 / lanes).astype(BF16))


def normalised(centered, gain, bias):
    spread = lane_means((centered * centered).astype(BF16))
    return (centered * lax.rsqrt(spread + 1e-05) * gain + bias).astype(BF16)


def gated(normed, weights):
    half_p = dot(normed, weights[0])
    return half_p + half_p * jnp.tanh(dot(normed, weights[1]))


def halved(w):
    return (w.astype(F32) * 0.5).astype(BF16)


def k_valid(mask_ref, first, columns, lanes):
    at = lax.broadcasted_iota(jnp.int32, (columns, lanes), 0)
    out = jnp.zeros((columns, lanes), F32)
    for n in range(columns):
        out = jnp.where(at == n, mask_ref[first + n].astype(F32), out)
    return out


def split_weights(we_ref, wg_ref):
    half = we_ref.shape[1] // 2
    left = halved(we_ref[:, :half]), halved(wg_ref[:, :half])
    right = halved(we_ref[:, half:]), halved(wg_ref[:, half:])
    return left, right


def contract(slabs, start, out, block, columns):
    at_once = min(32, block)
    for i in range(0, block, at_once):
        here = [pl.ds(j * block + i, at_once) for j in range(columns)]
        sums = [None if start is None else start[rows, :] for rows in here]
        for left_ref, right_ref in slabs:
            for k in range(columns):
                left = left_ref[pl.ds(i * columns + k, at_once, stride=columns), :]
                for j in range(columns):
                    term = left * right_ref[pl.ds(j * columns + k, 1), :]
                    sums[j] = term if sums[j] is None else sums[j] + term
        for rows, value in zip(here, sums):
            out[rows, :] = value.astype(out.dtype)


def block_rows(me, t, rows):
    return pl.ds(pl.multiple_of(((me // SQUARE) ^ t) * rows, rows), rows)


def right_edges(normed, weights, valids, refs):
    right = gated(normed, weights)
    columns, lanes = valids[0].shape
    js = normed.shape[0] // len(refs)
    for m, (valid, ref) in enumerate(zip(valids, refs)):
        ref[...] = (right[m * js : (m + 1) * js, :].reshape(columns, columns, lanes) * valid).reshape(js, lanes)


def place_rows(me, js):
    return pl.ds(pl.multiple_of((me % SQUARE) * js, js), js)


def edges_of(raws, lefts, rights, valids, gain, bias, weights, normed_ref, me, js):
    w_left, w_right = weights
    for m, x in enumerate(raws):
        normed_ref[m] = normalised(centred(x), gain, bias)
    for m in range(len(raws)):
        lefts[m][...] = gated(normed_ref[m], w_left)
    wanted = [m for m in range(len(raws)) if rights[m] is not None]
    if wanted:
        normed = jnp.concatenate([normed_ref[m, place_rows(me, js), :] for m in wanted], axis=0)
        right_edges(normed, w_right, [valids[m] for m in wanted], [rights[m] for m in wanted])


def own_kernel(squares, block, columns, *refs):
    me_ref, mask_ref, mask_row_ref, *refs = refs
    slabs, refs = refs[:2], refs[2:]
    gain_ref, bias_ref, we_ref, wg_ref, gate_ref, w_out_ref, out_gain_ref, out_bias_ref, *refs = refs
    gates_ref, far_valid_ref, i_valid_ref, j_valid_ref, w_copy_ref, norm_copy_ref, *refs = refs
    lefts, refs = refs[: 2 * squares], refs[2 * squares :]
    rights, refs = refs[: 2 * squares], refs[2 * squares :]
    shares, (normed_ref,) = refs[:-1], refs[-1:]
    me = me_ref[0]
    lanes = gates_ref.shape[1]
    rows, js = block * columns, columns * columns
    residues = mask_row_ref.shape[1]
    valids = [k_valid(mask_ref, (me ^ b) * columns, columns, lanes) for b in (0, CORE)]

    edges_of(
        [slab[block_rows(me, t, rows), :] for slab in slabs for t in range(squares)],
        lefts, rights, [valids[0]] * squares + [valids[1]] * squares,
        gain_ref[...], bias_ref[...], split_weights(we_ref, wg_ref), normed_ref, me, js,
    )
    half_gate = halved(gate_ref[...])
    for t in range(squares):
        gates_ref[t * rows : (t + 1) * rows, :] = 0.5 + 0.5 * jnp.tanh(dot(normed_ref[t], half_gate))
    for t in range(squares):
        for s in range(1, squares):
            terms = [(lefts[t], rights[s]), (lefts[squares + t], rights[squares + s])]
            contract(terms, None, shares[t * (squares - 1) + s - 1], block, columns)
    for n, bits in enumerate(FAR):
        far_valid_ref[n * columns : (n + 1) * columns, :] = k_valid(mask_ref, (me ^ bits) * columns, columns, lanes)
    j_valid_ref[...] = valids[0]
    for t in range(squares):
        at = lax.broadcasted_iota(jnp.int32, (block, residues), 0) + ((me // SQUARE) ^ t) * block
        chosen = jnp.where(lax.broadcasted_iota(jnp.int32, (block, residues), 1) == at, mask_row_ref[...], 0)
        i_valid_ref[t * block : (t + 1) * block, :] = dot(chosen.astype(F32).astype(BF16), jnp.ones((residues, lanes), BF16))
    w_copy_ref[...] = w_out_ref[...]
    norm_copy_ref[:1, :] = out_gain_ref[...]
    norm_copy_ref[1:, :] = out_bias_ref[...]


def piece_kernel(new, old, products, block, columns, *refs):
    refs = list(refs)

    def take(n):
        out = refs[:n]
        del refs[:n]
        return out

    rows, js = block * columns, columns * columns
    late = [p for p in old if p[1] == 0 and p[0] in FAR] if not new else []
    me = take(1)[0][0]
    raw = take(len(new) + len(late))
    valid_ref, gain_ref, bias_ref, we_ref, wg_ref = take(5)
    old_lefts, old_rights = take(len(old)), take(len(old) - len(late))
    starts = [take(1)[0] if begun else None for _, _, begun in products]
    made = [p for p in new if p[1]]
    new_lefts, new_rights = take(len(new)), take(len(made))
    outs = take(len(products))
    lefts = dict(zip(old, old_lefts))
    rights = dict(zip([p for p in old if p not in late], old_rights))
    weights = split_weights(we_ref, wg_ref)
    valid = lambda b: valid_ref[pl.ds(FAR.index(b) * columns, columns), :]
    if new:
        lefts.update(zip(new, new_lefts))
        rights.update(zip(made, new_rights))
        edges_of(
            [x[block_rows(me, t, rows) if x.shape[0] > rows else pl.ds(0, rows), :] for x, (_, t) in zip(raw, new)],
            new_lefts, [rights.get(p) for p in new], [valid(b) for b, _ in new],
            gain_ref[...], bias_ref[...], weights, refs[0], me, js,
        )
    if late:
        at = (me // SQUARE) * rows + (me % SQUARE) * js
        x = [x[pl.ds(pl.multiple_of(at, js), js) if x.shape[0] > rows else place_rows(me, js), :] for x in raw]
        normed = normalised(centred(jnp.concatenate(x, axis=0)), gain_ref[...], bias_ref[...])
        rights.update({p: refs[0].at[m] for m, p in enumerate(late)})
        right_edges(normed, weights[1], [valid(b) for b, _ in late], [rights[p] for p in late])
    for ((t, s), slabs, _), start, out in zip(products, starts, outs):
        contract([(lefts[b, t], rights[b, s]) for b in slabs], start, out, block, columns)
        if s == 0:
            out[...] = out[...] - two_part_means(out[...])


def last_kernel(t, n_sums, block, columns, me_ref, *refs):
    i_valid_ref, j_valid_ref, *refs = refs
    sums, refs = refs[:n_sums], refs[n_sums:]
    gates_ref, norm_ref, w_ref, *refs = refs
    out_ref, turned_ref = refs[-2:]
    rows = block * columns
    outer = sums[0][...]
    for other in sums[1:]:
        outer = outer + centred(other[...])
    i_valid = i_valid_ref[t * block : (t + 1) * block, :]
    outer = outer * jnp.concatenate([i_valid * j_valid_ref[j : j + 1, :] for j in range(columns)], axis=0)
    normed = normalised(outer, norm_ref[:1, :], norm_ref[1:, :])
    projected = dot(normed, w_ref[...])
    for j in range(columns):
        turned_ref[pl.ds(j, block, stride=columns), :] = projected[j * block : (j + 1) * block, :]
    out_ref[...] = (turned_ref[...] * gates_ref[t * rows : (t + 1) * rows, :]).astype(BF16)


def call(kernel, operands, smem, outs, scratch=()):
    return pl.pallas_call(
        kernel,
        out_shape=[jax.ShapeDtypeStruct(shape, dtype) for shape, dtype in outs],
        in_specs=[SMEM] * smem + [VMEM] * (len(operands) - smem),
        out_specs=[VMEM] * len(outs),
        scratch_shapes=list(scratch),
        compiler_params=pltpu.CompilerParams(vmem_limit_bytes=12 << 20),
    )(*operands)


def local(size, pair, residue_mask, ln_in_gain, ln_in_bias, w_edges, w_edge_gates, ln_out_gain, ln_out_bias, w_gate, w_out):
    residues, columns, lanes = pair.shape
    squares = size // SQUARE
    block = residues // squares
    rows, js = block * columns, columns * columns
    index = lax.axis_index("row")
    me = index.astype(jnp.int32).reshape(1)
    square = index // SQUARE

    def swap(value, bits):
        return lax.ppermute(value, "row", [(i, i ^ bits) for i in range(size)])

    in_gain, in_bias = ln_in_gain.reshape(1, lanes), ln_in_bias.reshape(1, lanes)
    flat = pair.reshape(residues * columns, lanes)
    order = list(range(1, squares)) + [0]
    raw = {}
    own = {t: lax.dynamic_slice_in_dim(pair, (square ^ t) * block, block, 0).reshape(rows, lanes) for t in order}

    def fetch(names, after=()):
        for b, t in names:
            raw[b, t] = swap(lax.optimization_barrier((own[t], after))[0] if len(after) else own[t], b)

    whole = swap(flat, CORNER)
    raw.update({(CORNER, t): whole for t in order})
    for t in order:
        fetch([(b, t) for b in (Z, Y)])
    near_whole = swap(flat, CORE)

    tile = lambda n, dtype=F32: ((n, lanes), dtype)
    with jax.named_scope("own_slab"):
        gates, far_valid, i_valid, j_valid, w_last, norm_last, *made = call(
            functools.partial(own_kernel, squares, block, columns),
            (me, residue_mask, residue_mask.reshape(1, residues), flat, near_whole, in_gain, in_bias, w_edges, w_edge_gates)
            + (w_gate, w_out, ln_out_gain.reshape(1, lanes), ln_out_bias.reshape(1, lanes)),
            2,
            [tile(squares * rows), tile(len(FAR) * columns), tile(squares * block), tile(columns), tile(lanes, BF16), tile(2)]
            + [tile(rows)] * (2 * squares) + [tile(js)] * (2 * squares) + [tile(rows)] * (squares * (squares - 1)),
            [pltpu.VMEM((2 * squares, rows, lanes), BF16)],
        )
    near = [(b, t) for b in (0, CORE) for t in range(squares)]
    lefts = dict(zip(near, made))
    rights = dict(zip(near, made[2 * squares :]))
    others = [(t, s) for t in range(squares) for s in range(1, squares)]
    sums = dict(zip(others, made[4 * squares :]))

    def pieces(new, products):
        read = sorted({(b, u) for (t, s), slabs, *_ in products for b in slabs for u in (t, s)} - set(new))
        late = [p for p in read if p not in rights]
        made = [p for p in new if p[1]]
        operands = [me] + [raw[p] for p in (*new, *late)] + [far_valid, in_gain, in_bias, w_edges, w_edge_gates]
        operands += [lefts[p] for p in read] + [rights[p] for p in read if p in rights]
        operands += [sums[ts] for ts, _, begun, _ in products if begun]
        scratch = pltpu.VMEM((len(new), rows, lanes), BF16) if new else pltpu.VMEM((len(late), js, lanes), F32)
        out = call(
            functools.partial(piece_kernel, tuple(new), tuple(read), tuple(p[:3] for p in products), block, columns),
            operands,
            1,
            [tile(rows)] * len(new) + [tile(js)] * len(made) + [tile(rows, dtype) for *_, dtype in products],
            [scratch],
        )
        lefts.update(zip(new, out))
        rights.update(zip(made, out[len(new) :]))
        return out[len(new) + len(made) :]

    def hand_on(names, after):
        for b, t in names:
            raw[b + CORE, t] = swap(lax.optimization_barrier((raw[b, t], after))[0], CORE)

    first, rest = order[0], order[1:]
    missing = {ts: set(FAR) for ts in others}
    arrived = {}

    def work(step):
        have = set(lefts) | set(step)
        products = []
        for (t, s), slabs in missing.items():
            now = tuple(b for b in FAR if b in slabs and (b, t) in have and (b, s) in have)
            if now:
                slabs -= set(now)
                products.append(((t, s), now, True, F32 if slabs else BF16))
        with jax.named_scope("pieces"):
            made = pieces(step, products)
        for ((t, s), *_, dtype), value in zip(products, made):
            if dtype == F32:
                sums[t, s] = value
            else:
                arrived[t ^ s, s] = swap(value, SQUARE * s)
        return lefts[step[-1]]

    hand_on([(Z, first), (Y, first)], gates)
    whole_of_core = swap(lax.optimization_barrier((whole, gates))[0], CORE)
    raw.update({(CORNER + CORE, t): whole_of_core for t in order})
    after = work([(Z, first), (Y, first), (CORNER, first)])
    for t in rest:
        hand_on([(b, t) for b in (Z, Y)], after)
    work([(b + CORE, first) for b in (Z, Y, CORNER)])
    for t in rest:
        work([(b, t) for b in FAR])
    with jax.named_scope("own_outer"):
        own_sums = pieces([], [((t, 0), (0, CORE, *FAR), False, F32) for t in range(squares)])

    update = None
    for t in range(squares):
        others = [arrived[t, s] for s in range(1, squares)]
        before = () if update is None else (update,)
        operands = (me, i_valid, j_valid, own_sums[t], *others, gates, norm_last, w_last, *before)
        with jax.named_scope("update"):
            update = pl.pallas_call(
                functools.partial(last_kernel, t, 1 + len(others), block, columns),
                out_shape=jax.ShapeDtypeStruct((residues * columns, lanes), BF16),
                grid_spec=pltpu.PrefetchScalarGridSpec(
                    num_scalar_prefetch=1,
                    grid=(1,),
                    in_specs=[VMEM] * (6 + len(others)) + [pl.BlockSpec(memory_space=pl.ANY)] * len(before),
                    out_specs=pl.BlockSpec((rows, lanes), lambda i, me_ref, t=t: ((me_ref[0] // SQUARE) ^ t, 0)),
                    scratch_shapes=[pltpu.VMEM((rows, lanes), F32)],
                ),
                input_output_aliases={len(operands) - 1: 0} if before else {},
                compiler_params=pltpu.CompilerParams(vmem_limit_bytes=12 << 20),
            )(*operands)
    return update.reshape(residues, columns, lanes)


def solution(mesh):
    return jax.shard_map(
        functools.partial(local, mesh.shape["row"]),
        mesh=mesh,
        in_specs=(P("groups", "row", None), P("groups"), P(), P(), P(), P(), P(), P(), P(), P()),
        out_specs=P("groups", "row", None),
        check_vma=False,
    )
```
